512 devices in a mesh: leaf: 64 (over z, x, core), panel: 8 (over y).
Axes of the slice: x: 4, y: 8, z: 8, core: 2. Of those that a mesh axis runs over, the one named last changes fastest.
Arguments:
- inverse_root: bfloat16 [2, 5120, 5120], P(None, 'panel', 'leaf'), may hold values from -0.0625 to 0.0625
- inverse_upper: bfloat16 [2, 5120, 10240], P(None, 'panel', 'leaf'), may hold values from -0.0625 to 0.0625
- inverse_middle: bfloat16 [2, 5120, 20480], P(None, 'panel', 'leaf'), may hold values from -0.0625 to 0.0625
- inverse_lower: bfloat16 [2, 5120, 40960], P(None, 'panel', 'leaf'), may hold values from -0.0625 to 0.0625
- coupling_upper: bfloat16 [2, 5120, 5120], P(None, 'leaf', 'panel'), may hold values from -0.0625 to 0.0625
- coupling_middle: bfloat16 [2, 10240, 5120], P(None, 'leaf', 'panel'), may hold values from -0.0625 to 0.0625
- coupling_lower: bfloat16 [2, 20480, 5120], P(None, 'leaf', 'panel'), may hold values from -0.0625 to 0.0625
- source_root: bfloat16 [2, 64, 5120], P(None, 'panel', 'leaf'), may hold values from -6 to 6
- source_upper: bfloat16 [2, 64, 10240], P(None, 'panel', 'leaf'), may hold values from -6 to 6
- source_middle: bfloat16 [2, 64, 20480], P(None, 'panel', 'leaf'), may hold values from -6 to 6
- source_lower: bfloat16 [2, 64, 40960], P(None, 'panel', 'leaf'), may hold values from -6 to 6
- blocks_upper: int32 [2, 20], replicated, may hold values from 0 to 39, as said below
- blocks_middle: int32 [4, 20], replicated, may hold values from 0 to 59, as said below
- blocks_lower: int32 [8, 20], replicated, may hold values from 0 to 59, as said below
- live_blocks: int32 [15], replicated, may hold values from 20 to 40, as said below
Outputs:
- answer_root: float32 [2, 64, 5120], P(None, 'panel', 'leaf')
- answer_upper: float32 [2, 64, 10240], P(None, 'panel', 'leaf')
- answer_middle: float32 [2, 64, 20480], P(None, 'panel', 'leaf')
- answer_lower: float32 [2, 64, 40960], P(None, 'panel', 'leaf')
The draws below stay inside these ranges and needn't reach their ends.
Inputs may be any that keep to these rules, and one draw needn't show every extreme that they name: `blocks_upper`: row f names 20 distinct blocks of the parent's front, whose blocks are the root's 40 pivot blocks; some row names the parent's first and last block. `blocks_middle`: row f names 20 distinct blocks of the parent's front (40 pivot blocks, then 20 update blocks); some row names the parent's first and last block. `blocks_lower`: row f names 20 distinct blocks of the parent's front (40 pivot blocks, then 20 update blocks); some row names the parent's first and last block. `live_blocks`: entry 2**l - 1 + f belongs to front f of level l; the root's entry is 40, and one front of level 3 has half of 40.
All inputs are finite; a program needn't handle non-finite values.
Results may differ from the reference program's by a relative error of at most 0.035.
Values may be sent and summed in bfloat16 or wider, within the bound.
No kernel may reach another device: no remote copies, remote signals or barrier semaphores. Data moves between devices by JAX's collectives and lax.ppermute only.
A program may use at most 128 MiB of HBM per device.

```python
import jax
import jax.numpy as jnp
from jax import lax

BLOCK = 128
P_SIZE = 5120
U = 2560
R = 64
PB = 40
UB = 20


def map_rows(key, fronts, block_total):
    subkeys = jax.random.split(key, fronts + 1)
    chosen = jax.random.randint(subkeys[fronts], (), 0, fronts)
    picked_rows = []
    for front_index in range(fronts):
        random_row = jax.random.permutation(subkeys[front_index], block_total)[:UB].astype(jnp.int32)
        middle_part = (1 + jax.random.permutation(subkeys[front_index], block_total - 2)[:UB - 2]).astype(jnp.int32)
        with_ends = jnp.concatenate([jnp.array([0, block_total - 1], dtype=jnp.int32), middle_part])
        picked_rows.append(jnp.where(chosen == front_index, with_ends, random_row))
    return jnp.stack(picked_rows)


def draw_blocks_upper(key, part):
    key = jax.random.fold_in(key, 11)
    return map_rows(key, 2, PB)


def draw_blocks_middle(key, part):
    key = jax.random.fold_in(key, 12)
    return map_rows(key, 4, PB + UB)


def draw_blocks_lower(key, part):
    key = jax.random.fold_in(key, 13)
    return map_rows(key, 8, PB + UB)


def draw_live_blocks(key, part):
    key = jax.random.fold_in(key, 14)
    count_key, place_key = jax.random.split(key)
    counts = jax.random.randint(count_key, (15,), PB // 2, PB + 1)
    lowest = jax.random.randint(place_key, (), 7, 15)
    entries = jnp.arange(15)
    counts = jnp.where(entries == 0, PB, counts)
    counts = jnp.where(entries == lowest, PB // 2, counts)
    return counts.astype(jnp.int32)


def block_levels(key, dims, cuts, smallest, top_value):
    factor_of, own = 1.0, jax.random.fold_in(key, 6)
    for axis_at, blocks in cuts:
        steps = jnp.exp(jax.random.uniform(jax.random.fold_in(own, axis_at), (blocks,), jnp.float32, smallest / len(cuts), top_value / len(cuts)))
        factor_of = factor_of * jnp.repeat(steps, dims[axis_at] // blocks).reshape([-1 if axis == axis_at else 1 for axis in range(len(dims))])
    return factor_of


def gaussian(key, shape, width, bound, shards=(), held_as=jnp.bfloat16):
    factor_of = block_levels(key, shape, shards, -0.22, 0.18) if shards else 1.0
    drawn = jax.random.normal(key, shape, jnp.float32) * width * factor_of
    return jnp.minimum(jnp.maximum(drawn, -bound), bound).astype(held_as)


def setup_inputs(seed: int = 0) -> dict:
    key_of = jax.random.split(jax.random.key(seed), 16)
    return {
        "inverse_root": gaussian(key_of[0], (2, P_SIZE, P_SIZE), (2 * P_SIZE) ** -0.5, 0.0625, ((1, 8), (2, 64))),
        "inverse_upper": gaussian(key_of[1], (2, P_SIZE, 2 * P_SIZE), (2 * P_SIZE) ** -0.5, 0.0625, ((1, 8), (2, 64))),
        "inverse_middle": gaussian(key_of[2], (2, P_SIZE, 4 * P_SIZE), (2 * P_SIZE) ** -0.5, 0.0625, ((1, 8), (2, 64))),
        "inverse_lower": gaussian(key_of[3], (2, P_SIZE, 8 * P_SIZE), (2 * P_SIZE) ** -0.5, 0.0625, ((1, 8), (2, 64))),
        "coupling_upper": gaussian(key_of[4], (2, 2 * U, P_SIZE), (2 * P_SIZE) ** -0.5, 0.0625, ((1, 64), (2, 8))),
        "coupling_middle": gaussian(key_of[5], (2, 4 * U, P_SIZE), (2 * P_SIZE) ** -0.5, 0.0625, ((1, 64), (2, 8))),
        "coupling_lower": gaussian(key_of[6], (2, 8 * U, P_SIZE), (2 * P_SIZE) ** -0.5, 0.0625, ((1, 64), (2, 8))),
        "source_root": gaussian(key_of[7], (2, R, P_SIZE), 1.0, 6.0, ((1, 8), (2, 64))),
        "source_upper": gaussian(key_of[8], (2, R, 2 * P_SIZE), 1.0, 6.0, ((1, 8), (2, 64))),
        "source_middle": gaussian(key_of[9], (2, R, 4 * P_SIZE), 1.0, 6.0, ((1, 8), (2, 64))),
        "source_lower": gaussian(key_of[10], (2, R, 8 * P_SIZE), 1.0, 6.0, ((1, 8), (2, 64))),
        "blocks_upper": draw_blocks_upper(jax.random.fold_in(key_of[15], 71), 0),
        "blocks_middle": draw_blocks_middle(jax.random.fold_in(key_of[15], 71), 0),
        "blocks_lower": draw_blocks_lower(jax.random.fold_in(key_of[15], 71), 0),
        "live_blocks": draw_live_blocks(jax.random.fold_in(key_of[15], 71), 0),
    }


def conj_apply(matrix, vector):
    real_one = jnp.dot(vector[0], matrix[0].T, preferred_element_type=jnp.float32)
    real_two = jnp.dot(vector[1], matrix[1].T, preferred_element_type=jnp.float32)
    imag_one = jnp.dot(vector[1], matrix[0].T, preferred_element_type=jnp.float32)
    imag_two = jnp.dot(vector[0], matrix[1].T, preferred_element_type=jnp.float32)
    return jnp.stack([real_one + real_two, imag_one - imag_two])


def herm_apply(matrix, vector):
    real_one = jnp.dot(vector[0], matrix[0], preferred_element_type=jnp.float32)
    real_two = jnp.dot(vector[1], matrix[1], preferred_element_type=jnp.float32)
    imag_one = jnp.dot(vector[1], matrix[0], preferred_element_type=jnp.float32)
    imag_two = jnp.dot(vector[0], matrix[1], preferred_element_type=jnp.float32)
    return jnp.stack([real_one + real_two, imag_one - imag_two])


def front_mask(live_count):
    row_ids = jnp.arange(P_SIZE, dtype=jnp.int32)
    return ((row_ids // BLOCK) < live_count).astype(jnp.float32)


def reference(inverse_root, inverse_upper, inverse_middle, inverse_lower,
              coupling_upper, coupling_middle, coupling_lower,
              source_root, source_upper, source_middle, source_lower,
              blocks_upper, blocks_middle, blocks_lower, live_blocks):
    inverses = (inverse_root, inverse_upper, inverse_middle, inverse_lower)
    couplings = (None, coupling_upper, coupling_middle, coupling_lower)
    sources = (source_root, source_upper, source_middle, source_lower)
    tables = (None, blocks_upper, blocks_middle, blocks_lower)
    count_rhs = source_root.shape[1]
    solved = {}
    outgoing = {}
    for level_index in (3, 2, 1, 0):
        for front_index in range(1 << level_index):
            row_mask = front_mask(live_blocks[(1 << level_index) - 1 + front_index])
            matrix = inverses[level_index][:, :, front_index * P_SIZE:(front_index + 1) * P_SIZE]
            source = sources[level_index][:, :, front_index * P_SIZE:(front_index + 1) * P_SIZE].astype(jnp.float32)
            passed = None
            if level_index == 3:
                reduced = source * row_mask
            else:
                block_count = P_SIZE // BLOCK + (U // BLOCK if level_index >= 1 else 0)
                child_pair = tables[level_index + 1][2 * front_index:2 * front_index + 2]
                children = jnp.stack([outgoing[(level_index + 1, 2 * front_index)],
                                      outgoing[(level_index + 1, 2 * front_index + 1)]], 2)
                pieces = children.astype(jnp.float32).reshape(2, count_rhs, 2, U // BLOCK, BLOCK)
                select = (child_pair[:, :, None] == jnp.arange(block_count, dtype=jnp.int32)[None, None, :]).astype(jnp.float32)
                assembled = jnp.einsum("crhbx,hbk->crkx", pieces, select, precision=lax.Precision.HIGHEST)
                assembled = assembled.reshape(2, count_rhs, block_count * BLOCK)
                reduced = (source - assembled[:, :, :P_SIZE]) * row_mask
                if level_index >= 1:
                    passed = assembled[:, :, P_SIZE:]
            solved_rows = (conj_apply(matrix, reduced.astype(jnp.bfloat16)) * row_mask).astype(jnp.bfloat16)
            solved[(level_index, front_index)] = solved_rows
            if level_index >= 1:
                coupling = couplings[level_index][:, front_index * U:(front_index + 1) * U, :]
                update = conj_apply(coupling, solved_rows)
                if passed is not None:
                    update = update + passed
                outgoing[(level_index, front_index)] = update.astype(jnp.bfloat16)
    values = {}
    results = []
    for level_index in (0, 1, 2, 3):
        pieces_out = []
        for front_index in range(1 << level_index):
            row_mask = front_mask(live_blocks[(1 << level_index) - 1 + front_index])
            matrix = inverses[level_index][:, :, front_index * P_SIZE:(front_index + 1) * P_SIZE]
            picked = None
            if level_index == 0:
                target = solved[(0, 0)]
            else:
                front_values = values[(level_index - 1, front_index // 2)]
                block_count = front_values.shape[2] // BLOCK
                map_row = tables[level_index][front_index]
                select = (map_row[:, None] == jnp.arange(block_count, dtype=jnp.int32)[None, :]).astype(jnp.float32)
                picked = jnp.einsum("crkx,bk->crbx",
                                    front_values.astype(jnp.float32).reshape(2, count_rhs, block_count, BLOCK),
                                    select, precision=lax.Precision.HIGHEST)
                picked = picked.reshape(2, count_rhs, U).astype(jnp.bfloat16)
                coupling = couplings[level_index][:, front_index * U:(front_index + 1) * U, :]
                target = (solved[(level_index, front_index)].astype(jnp.float32)
                          - herm_apply(coupling, picked)).astype(jnp.bfloat16)
            answer = herm_apply(matrix, target) * row_mask
            pieces_out.append(answer)
            outgoing_values = answer.astype(jnp.bfloat16)
            if picked is not None:
                outgoing_values = jnp.concatenate([outgoing_values, picked], 2)
            values[(level_index, front_index)] = outgoing_values
        results.append(jnp.concatenate(pieces_out, 2))
    return results[0], results[1], results[2], results[3]
```

```python
import functools

import jax
import jax.numpy as jnp
from jax import lax
from jax.experimental import pallas as pl
from jax.experimental.pallas import tpu as pltpu
from jax.sharding import Mesh
from jax.sharding import PartitionSpec as P

BLOCK = 128
P_SIZE = 5120
U = 2560
PANELS = 8
SHARES = 8
PIVOT_BLOCKS = P_SIZE // BLOCK
UPDATE_BLOCKS = U // BLOCK
ROWS = P_SIZE // PANELS
WIDE = 128

LEAF = ("z2", "z1", "z0", "x", "c")
SHARE = ("x", "c")
DEPTH = ("z2", "z1", "z0")


def exchange(value, axes):
    return lax.all_to_all(value, axes, 0, 0, tiled=True)


def scatter_sum(value, axes):
    return jnp.sum(exchange(value.astype(jnp.bfloat16), axes).astype(jnp.float32), 0)


def gather(value, axes, count):
    return exchange(jnp.broadcast_to(value[None], (count,) + value.shape), axes)


def partner(value):
    return lax.ppermute(value, "z0", [(0, 1), (1, 0)])


def halves(vector):
    half = vector.shape[0] // 2
    other = jnp.concatenate([vector[half:], -vector[:half]], 0)
    return vector.astype(jnp.bfloat16), other.astype(jnp.bfloat16)


def multiply(pieces, matrix_ref, start, span, contract):
    dims = (((1,), (contract,)), ((), ()))
    total = None
    for part, piece in enumerate(pieces):
        matrix = matrix_ref[start : start + span, part].reshape(ROWS, ROWS)
        term = lax.dot_general(piece, matrix, dims, preferred_element_type=jnp.float32)
        total = term if total is None else total + term
    return total


def bring(pack_ref, matrix_ref, sems, rows, offset):
    copies = []
    for share in range(SHARES):
        copies.append(
            pltpu.make_async_copy(
                pack_ref.at[share, :, pl.ds(offset * rows, rows)],
                matrix_ref.at[share],
                sems.at[share],
            )
        )
    for copy in copies:
        copy.start()
    return copies


def take_block(index_ref, held_ref, place):
    per = held_ref.shape[2] // BLOCK
    total = None
    for term in range(index_ref.shape[0]):
        spot = index_ref[term, place]
        safe = jnp.maximum(spot, 0)
        start = pl.multiple_of((safe % per) * BLOCK, BLOCK)
        block = held_ref[safe // per, :, pl.ds(start, BLOCK)].astype(jnp.float32)
        block = jnp.where(spot >= 0, block, 0.0)
        total = block if total is None else total + block
    return total


def params():
    return pltpu.CompilerParams(vmem_limit_bytes=24 * 2**20)


def smem():
    return pl.BlockSpec(memory_space=pltpu.SMEM)


def vmem():
    return pl.BlockSpec(memory_space=pltpu.VMEM)


def hbm():
    return pl.BlockSpec(memory_space=pltpu.HBM)


def in_hbm(value):
    return pltpu.with_memory_space_constraint(value, pltpu.HBM)


def matrix_scratch(rows):
    return [
        pltpu.VMEM((SHARES, 2, rows, ROWS), jnp.bfloat16),
        pltpu.SemaphoreType.DMA((SHARES,)),
    ]


def columns_kernel(rows, offset, updates, has_held, has_base, keep, *refs):
    refs = list(refs)
    index_ref = refs.pop(0) if has_held else None
    live_ref = refs.pop(0) if has_base and has_held else None
    held_ref = refs.pop(0) if has_held else None
    base_ref = refs.pop(0) if has_base else None
    pack_ref = refs.pop(0)
    out_ref = refs.pop(0)
    passed_ref = refs.pop(0) if updates else None
    keep_ref = refs.pop(0) if keep else None
    matrix_ref, sems = refs
    copies = bring(pack_ref, matrix_ref, sems, rows, offset)
    steps = SHARES * rows // ROWS
    span = ROWS // BLOCK
    group = ROWS // rows
    total = None
    for step in range(steps):
        if has_held:
            blocks = []
            for place in range(step * span, (step + 1) * span):
                block = take_block(index_ref, held_ref, place)
                if has_base:
                    base = base_ref[:, place * BLOCK : (place + 1) * BLOCK].astype(jnp.float32)
                    block = jnp.where(place < live_ref[0], base - block, 0.0)
                blocks.append(block)
            vector = jnp.concatenate(blocks, 1)
        else:
            vector = base_ref[:, step * ROWS : (step + 1) * ROWS].astype(jnp.float32)
        if keep:
            keep_ref[:, step * ROWS : (step + 1) * ROWS] = vector.astype(jnp.bfloat16)
        for share in range(step * group, (step + 1) * group):
            copies[share].wait()
        term = multiply(halves(vector), matrix_ref, step * group, group, 0)
        total = term if total is None else total + term
    for place in range(updates):
        passed_ref[:, place * BLOCK : (place + 1) * BLOCK] = take_block(
            index_ref, held_ref, steps * span + place
        )
    result = total.astype(out_ref.dtype)
    for copy in range(out_ref.shape[0]):
        out_ref[copy] = result


def over_columns(
    pack, rows, offset, copies, index=None, held=None, live=None, base=None,
    keep=False, dtype=jnp.bfloat16,
):
    steps = SHARES * rows // ROWS
    updates = index.shape[1] - steps * (ROWS // BLOCK) if index is not None else 0
    args, specs = [], []
    if held is not None:
        args.append(index)
        specs.append(smem())
        if base is not None:
            args.append(live)
            specs.append(smem())
        args.append(held)
        specs.append(vmem())
    if base is not None:
        args.append(base)
        specs.append(vmem())
    args.append(in_hbm(pack))
    specs.append(hbm())
    shapes = [jax.ShapeDtypeStruct((copies, 16, ROWS), dtype)]
    if updates:
        shapes.append(jax.ShapeDtypeStruct((16, updates * BLOCK), jnp.float32))
    if keep:
        shapes.append(jax.ShapeDtypeStruct((16, steps * ROWS), jnp.bfloat16))
    return pl.pallas_call(
        functools.partial(
            columns_kernel, rows, offset, updates, held is not None, base is not None, keep
        ),
        out_shape=shapes,
        in_specs=specs,
        out_specs=[vmem()] * len(shapes),
        scratch_shapes=matrix_scratch(rows),
        compiler_params=params(),
    )(*args)


def rows_kernel(rows, offset, parts, masked, *refs):
    refs = list(refs)
    live_ref = refs.pop(0) if masked else None
    part_refs = [refs.pop(0) for _ in range(parts)]
    held_ref = None if masked else refs.pop(0)
    pack_ref = refs.pop(0)
    out_ref = refs.pop(0)
    keep_ref = refs.pop(0) if masked else None
    matrix_ref, sems = refs
    copies = bring(pack_ref, matrix_ref, sems, rows, offset)
    total = None
    for part_ref in part_refs:
        for copy in range(part_ref.shape[0]):
            term = part_ref[copy].astype(jnp.float32)
            total = term if total is None else total + term
    if masked:
        place = lax.broadcasted_iota(jnp.int32, total.shape, 1) // BLOCK
        total = jnp.where(place < live_ref[0], total, 0.0)
        keep_ref[...] = total.astype(jnp.bfloat16)
    else:
        total = held_ref[...].astype(jnp.float32) - total
    pieces = halves(total)
    group = ROWS // rows
    for step in range(SHARES // group):
        for share in range(step * group, (step + 1) * group):
            copies[share].wait()
        result = multiply(pieces, matrix_ref, step * group, group, 1).astype(jnp.bfloat16)
        for copy in range(out_ref.shape[0]):
            out_ref[copy, :, step * ROWS : (step + 1) * ROWS] = result


def over_rows(pack, rows, offset, copies, parts, live=None, held=None):
    masked = live is not None
    args = ([live] if masked else []) + list(parts) + ([] if masked else [held]) + [in_hbm(pack)]
    specs = ([smem()] if masked else []) + [vmem()] * len(parts)
    specs += ([] if masked else [vmem()]) + [hbm()]
    shapes = [jax.ShapeDtypeStruct((copies, 16, SHARES * rows), jnp.bfloat16)]
    if masked:
        shapes.append(jax.ShapeDtypeStruct((16, ROWS), jnp.bfloat16))
    return pl.pallas_call(
        functools.partial(rows_kernel, rows, offset, len(parts), masked),
        out_shape=shapes,
        in_specs=specs,
        out_specs=[vmem()] * len(shapes),
        scratch_shapes=matrix_scratch(rows),
        compiler_params=params(),
    )(*args)


def crossed(vector):
    row = lax.broadcasted_iota(jnp.int32, (64, 64), 0)
    column = lax.broadcasted_iota(jnp.int32, (64, 64), 1)
    up = (column == row + 1) & (row % 2 == 0)
    down = (column == row - 1) & (row % 2 == 1)
    turn = jnp.where(up, 1.0, jnp.where(down, -1.0, 0.0)).astype(jnp.bfloat16)
    return jnp.dot(turn, vector, preferred_element_type=jnp.float32).astype(jnp.bfloat16)


def pair_dot(vector, other, matrix):
    dims = (((1,), (1,)), ((), ()))
    one = lax.dot_general(vector, matrix[0], dims, preferred_element_type=jnp.float32)
    return one + lax.dot_general(other, matrix[1], dims, preferred_element_type=jnp.float32)


def fetch(own_ref, matrix_ref, sem):
    copy = pltpu.make_async_copy(own_ref, matrix_ref, sem)
    copy.start()
    return copy


def lower_pivots_kernel(
    info_ref, every_ref, own_ref, other_ref, out_ref, matrix_ref, sem
):
    fetched = fetch(own_ref, matrix_ref, sem)
    place = lax.broadcasted_iota(jnp.int32, (64, ROWS), 1) // BLOCK
    sides = []
    for side in range(2):
        value = every_ref[side * 64 : (side + 1) * 64, :ROWS].astype(jnp.float32)
        sides.append(jnp.where(place + side * (ROWS // BLOCK) < info_ref[0], value, 0.0))
    even = info_ref[1] == 0
    vectors = (jnp.where(even, sides[0], sides[1]), jnp.where(even, sides[1], sides[0]))
    row = lax.broadcasted_iota(jnp.int32, (128, 128), 0)
    source = (row % 2) * 64 + (row // 2 % 8) * 8 + (row // 32) * 2 + row // 16 % 2
    order = (lax.broadcasted_iota(jnp.int32, (128, 128), 1) == source).astype(jnp.bfloat16)
    extra = jnp.dot(order, every_ref[:, ROWS:], preferred_element_type=jnp.float32)
    extra = extra.astype(jnp.bfloat16)
    total = None
    for side in (1, 0):
        vector = vectors[side].astype(jnp.bfloat16)
        if side == 0:
            fetched.wait()
        term = pair_dot(vector, crossed(vector), (matrix_ref, other_ref)[side])
        total = term if total is None else total + term
    total = total.astype(jnp.bfloat16)
    for copy in range(4):
        out_ref[copy, :64] = total
        out_ref[copy, 64:] = extra[copy * 32 : (copy + 1) * 32]


def lower_pivots(info, every, own, other):
    return pl.pallas_call(
        lower_pivots_kernel,
        out_shape=jax.ShapeDtypeStruct((4, 96, ROWS), jnp.bfloat16),
        in_specs=[smem(), vmem(), hbm(), vmem()],
        out_specs=vmem(),
        scratch_shapes=[
            pltpu.VMEM(own.shape, jnp.bfloat16),
            pltpu.SemaphoreType.DMA,
        ],
        compiler_params=params(),
    )(info, every, in_hbm(own), other)


def lower_updates_kernel(
    info_ref, got_ref, own_ref, other_ref, out_ref, solved_ref, matrix_ref, sem
):
    fetched = fetch(own_ref, matrix_ref, sem)
    total = None
    for copy in range(4):
        term = got_ref[copy, :64].astype(jnp.float32)
        total = term if total is None else total + term
    place = lax.broadcasted_iota(jnp.int32, (64, ROWS), 1) // BLOCK
    vector = jnp.where(place < info_ref[0], total, 0.0).astype(jnp.bfloat16)
    solved_ref[...] = vector
    row = lax.broadcasted_iota(jnp.int32, (64, 64), 0)
    source = (row // 2 % 8) * 8 + (row // 16) * 2 + row % 2
    order = (lax.broadcasted_iota(jnp.int32, (64, 64), 1) == source).astype(jnp.bfloat16)
    vector = jnp.dot(order, vector, preferred_element_type=jnp.float32).astype(jnp.bfloat16)
    turn = crossed(vector)
    other = pair_dot(vector, turn, other_ref)
    fetched.wait()
    sides = [pair_dot(vector, turn, matrix_ref), other]
    even = info_ref[1] == 0
    own = sides[0].shape[1]
    first = jnp.where(even, sides[0], sides[1]).astype(jnp.bfloat16)
    second = jnp.where(even, sides[1], sides[0]).astype(jnp.bfloat16)
    for copy in range(2):
        out_ref[copy, :, :own] = first
        out_ref[copy, :, own:] = second


def lower_updates(info, got, own, other):
    return pl.pallas_call(
        lower_updates_kernel,
        out_shape=[
            jax.ShapeDtypeStruct((2, 64, ROWS), jnp.bfloat16),
            jax.ShapeDtypeStruct((64, ROWS), jnp.bfloat16),
        ],
        in_specs=[smem(), vmem(), hbm(), vmem()],
        out_specs=[vmem()] * 2,
        scratch_shapes=[
            pltpu.VMEM(own.shape, jnp.bfloat16),
            pltpu.SemaphoreType.DMA,
        ],
        compiler_params=params(),
    )(info, got, in_hbm(own), other)


def hand_kernel(masked, added, tailed, *refs):
    refs = list(refs)
    live_ref = refs.pop(0) if masked else None
    part_ref = refs.pop(0)
    more_ref = refs.pop(0) if added else None
    tail_ref = refs.pop(0) if tailed else None
    out_ref = refs.pop(0)
    total = part_ref[0].astype(jnp.float32)
    for copy in range(1, part_ref.shape[0]):
        total = total + part_ref[copy].astype(jnp.float32)
    if added:
        total = total + more_ref[...]
    if masked:
        place = lax.broadcasted_iota(jnp.int32, total.shape, 1) // BLOCK
        total = jnp.where(place < live_ref[0], total, 0.0)
    total = total.astype(jnp.bfloat16)
    for copy in range(out_ref.shape[0]):
        out_ref[copy, :, : total.shape[1]] = total
        if tailed:
            out_ref[copy, :, total.shape[1] :] = tail_ref[...]


def hand_on(part, copies, live=None, more=None, tail=None):
    width = part.shape[2] + (tail.shape[1] if tail is not None else 0)
    args = [item for item in (live, part, more, tail) if item is not None]
    specs = [smem()] * (live is not None) + [vmem()] * (len(args) - (live is not None))
    return pl.pallas_call(
        functools.partial(hand_kernel, live is not None, more is not None, tail is not None),
        out_shape=jax.ShapeDtypeStruct((copies, 16, width), jnp.bfloat16),
        in_specs=specs,
        out_specs=vmem(),
        compiler_params=params(),
    )(*args)


def pick_kernel(index_ref, held_ref, out_ref):
    for place in range(index_ref.shape[1]):
        out_ref[:, place * BLOCK : (place + 1) * BLOCK] = take_block(index_ref, held_ref, place)


def take_blocks(index, held):
    return pl.pallas_call(
        pick_kernel,
        out_shape=jax.ShapeDtypeStruct((held.shape[1], index.shape[1] * BLOCK), jnp.float32),
        in_specs=[smem(), pl.BlockSpec(memory_space=pltpu.VMEM)],
        out_specs=pl.BlockSpec(memory_space=pltpu.VMEM),
        compiler_params=params(),
    )(index, held)


def last_kernel(got_ref, own_ref, out_ref, matrix_ref, sem):
    fetched = fetch(own_ref, matrix_ref, sem)
    stacked = jnp.concatenate([got_ref[share, :16] for share in range(SHARES)], 0)
    row = lax.broadcasted_iota(jnp.int32, (WIDE, WIDE), 0)
    column = lax.broadcasted_iota(jnp.int32, (WIDE, WIDE), 1)
    total = None
    for part in range(2):
        imaginary = (row // 8 + part) % 2
        source = row % 8 * 16 + imaginary * 8 + row // 16
        sign = jnp.where((row // 8 % 2 == 1) & (part == 1), -1.0, 1.0)
        order = jnp.where(column == source, sign, 0.0).astype(jnp.bfloat16)
        vector = jnp.dot(order, stacked, preferred_element_type=jnp.float32)
        if part == 0:
            fetched.wait()
        term = jnp.dot(
            vector.astype(jnp.bfloat16), matrix_ref[part], preferred_element_type=jnp.float32
        )
        total = term if total is None else total + term
    out_ref[...] = total.astype(jnp.bfloat16)


def last_product(got, own):
    return pl.pallas_call(
        last_kernel,
        out_shape=jax.ShapeDtypeStruct((WIDE, ROWS), jnp.bfloat16),
        in_specs=[vmem(), hbm()],
        out_specs=vmem(),
        scratch_shapes=[pltpu.VMEM(own.shape, jnp.bfloat16), pltpu.SemaphoreType.DMA],
        compiler_params=params(),
    )(got, in_hbm(own))


def shards(
    inverse_root,
    inverse_upper,
    inverse_middle,
    inverse_lower,
    coupling_upper,
    coupling_middle,
    coupling_lower,
    source_root,
    source_upper,
    source_middle,
    source_lower,
    blocks_upper,
    blocks_middle,
    blocks_lower,
    live_blocks,
):
    tables = (None, blocks_upper, blocks_middle, blocks_lower)
    sources = (source_root, source_upper, source_middle, source_lower)
    depth = lax.axis_index(DEPTH)
    share = lax.axis_index(SHARE)
    column = lax.axis_index("panel")

    packs = [
        jnp.concatenate([inverse_middle.swapaxes(1, 2), coupling_middle], 1),
        jnp.concatenate(
            [inverse_upper.swapaxes(1, 2), coupling_upper, inverse_root.swapaxes(1, 2)], 1
        ),
        coupling_lower,
    ]
    packs = [lax.all_gather(pack, SHARE, axis=0, tiled=False) for pack in packs]
    pivot_at = {2: (packs[0], 320, 0), 1: (packs[1], 160, 0), 0: (packs[1], 80, 3)}
    update_at = {2: (packs[0], 160, 2), 1: (packs[1], 80, 2)}

    def front_of(level):
        width = 8 >> level
        return depth // width, depth % width

    def live_of(level):
        front, _ = front_of(level)
        return lax.dynamic_slice_in_dim(live_blocks, (1 << level) - 1 + front, 1, 0)[0]

    def panel_live(level):
        return (live_of(level) - column * (ROWS // BLOCK))[None]

    def depth_live(level):
        return (live_of(level) - front_of(level)[1] * (PIVOT_BLOCKS // (8 >> level)))[None]

    def incoming(level):
        front, within = front_of(level)
        pair = lax.dynamic_slice_in_dim(tables[level + 1], 2 * front, 2, 0)
        pivots = PIVOT_BLOCKS // (8 >> level)
        goal = within * pivots + jnp.arange(pivots, dtype=jnp.int32)
        if level >= 1:
            updates = UPDATE_BLOCKS // (8 >> level)
            extra = PIVOT_BLOCKS + within * updates + jnp.arange(updates, dtype=jnp.int32)
            goal = jnp.concatenate([goal, extra])
        order = jnp.arange(2 * UPDATE_BLOCKS, dtype=jnp.int32).reshape(2, 1, UPDATE_BLOCKS)
        match = pair[:, None, :] == goal[None, :, None]
        return jnp.max(jnp.where(match, order, -1), 2)

    def picking(level, complete=False):
        front, within = front_of(level)
        parts = 16 >> level
        pivots = PIVOT_BLOCKS // parts
        updates = UPDATE_BLOCKS // parts if level >= 2 else 0
        own = UPDATE_BLOCKS // (8 >> level)
        row = lax.dynamic_slice_in_dim(tables[level], front, 1, 0)[0]
        if not complete:
            row = lax.dynamic_slice_in_dim(row, within * own, own, 0)
        whole = pivots + updates
        spot = row // pivots * whole + row % pivots
        if updates:
            rest = row - PIVOT_BLOCKS
            spot = jnp.where(rest >= 0, rest // updates * whole + pivots + rest % updates, spot)
        return spot[None]

    def handing():
        row = lax.dynamic_slice_in_dim(tables[3], depth, 1, 0)
        pivots = PIVOT_BLOCKS // 2
        updates = UPDATE_BLOCKS // 2
        rest = row - PIVOT_BLOCKS
        later = rest // updates * (pivots + updates) + pivots + rest % updates
        return jnp.where(rest >= 0, later, row // pivots * (pivots + updates) + row % pivots)

    core = lax.axis_index("c")
    other_inverse = lax.ppermute(inverse_lower, "c", [(0, 1), (1, 0)])
    other_coupling = lax.ppermute(coupling_lower, "c", [(0, 1), (1, 0)])
    packed = [source_lower] + [sources[level] for level in (2, 1, 0)]
    widths = [piece.shape[2] for piece in packed[1:]]
    packed = jnp.concatenate(packed, 2)
    packed = jnp.pad(packed, ((0, 0), (0, 0), (0, 2 * ROWS - packed.shape[2])))
    packed = packed.reshape(2, 4, 2, 2 * ROWS).transpose(2, 1, 0, 3).reshape(2, 1, 8, 2 * ROWS)
    packed = jnp.broadcast_to(packed, (2, PANELS, 8, 2 * ROWS)).reshape(16, 8, 2 * ROWS)
    every = exchange(packed, ("c", "panel")).reshape(WIDE, 2 * ROWS)
    place = lax.axis_index("x") * 2
    span = ROWS // BLOCK
    info = jnp.stack([live_of(3) - place * span, core])
    partial = lower_pivots(info, every, inverse_lower, other_inverse)
    got = exchange(partial, "x")
    info = jnp.stack([live_of(3) - column * span, core])
    update, solved = lower_updates(info, got, coupling_lower, other_coupling)
    solved_mine = lax.dynamic_slice_in_dim(
        solved.reshape(PANELS, 4, 2, ROWS), lax.axis_index("x"), 1, 1
    )
    solved_mine = solved_mine[:, 0].transpose(1, 0, 2).reshape(16, ROWS)

    children = exchange(update.reshape(64, 2, ROWS), ("z0", "x", "panel"))
    children = children.reshape(8, PANELS, 2, ROWS).astype(jnp.float32)
    children = jnp.sum(children, 1).astype(jnp.bfloat16)
    children = children.transpose(1, 0, 2).reshape(2, P_SIZE)
    spread = gather(children, "panel", PANELS).transpose(1, 0, 2).reshape(16, P_SIZE)
    gathered = spread[None]
    base = {}
    start = 0
    extra = got[:, 64:].reshape(4, 16, 2, ROWS).transpose(1, 0, 2, 3)
    for level, width in zip((2, 1, 0), widths):
        base[level] = extra[:, :, :, start : start + width].reshape(16, SHARES * width)
        start += width

    held = {}
    for level in (2, 1, 0):
        count = 8 >> level
        found = over_columns(
            *pivot_at[level],
            1 if level == 2 else count,
            index=incoming(level),
            held=gathered,
            live=depth_live(level),
            base=base[level],
        )
        if level == 2:
            parts = [found[0], partner(found[0])]
        else:
            parts = [exchange(found[0], DEPTH[level:])]
        if level >= 1:
            update, held[level] = over_rows(
                *update_at[level], PANELS, parts, live=panel_live(level)
            )
            update = hand_on(exchange(update, "panel"), 2 * count, more=found[1])
            gathered = exchange(update, DEPTH[level - 1 :])

    answers = []
    picked = None
    for level in (0, 1, 2):
        count = 8 >> level
        if level == 0:
            answer, _ = over_rows(*pivot_at[0], PANELS, parts, live=panel_live(0))
        else:
            partial, picked = over_columns(
                *update_at[level],
                1 if level == 2 else count,
                index=picking(level),
                held=gathered,
                keep=True,
            )
            if level == 2:
                parts = [partial, partner(partial)]
            else:
                parts = [exchange(partial, DEPTH[level:])]
            (answer,) = over_rows(
                *pivot_at[level], 1 if level == 2 else PANELS, parts, held=held[level]
            )
        if level < 2:
            outgoing = hand_on(
                exchange(answer, "panel"), count, live=depth_live(level), tail=picked
            )
            mine = outgoing[0, :, : P_SIZE // count].reshape(2, PANELS, -1)
            answers.append(lax.dynamic_slice_in_dim(mine, column, 1, 1)[:, 0])
            gathered = exchange(outgoing, DEPTH[level:])
        else:
            answer = answer.reshape(2, PANELS, -1).transpose(1, 0, 2)
            answer = exchange(jnp.concatenate([answer, answer], 0), ("z0", "panel"))
            answer = answer.reshape(2, PANELS, 2, -1).astype(jnp.float32)
            row_mask = (jnp.arange(P_SIZE, dtype=jnp.int32) // BLOCK < live_of(2)).reshape(2, 1, -1)
            both = (jnp.sum(answer, 1) * row_mask).astype(jnp.bfloat16)
            answers.append(lax.dynamic_slice_in_dim(both, front_of(2)[1], 1, 0)[0])

    passed = take_blocks(picking(2, True), gathered).reshape(2, PANELS, 2, -1)
    passed = lax.dynamic_slice_in_dim(passed, column, 1, 1)[:, 0].transpose(1, 0, 2)
    both = jnp.concatenate([both.astype(jnp.float32), passed], 2)
    handed = take_blocks(handing(), both).astype(jnp.bfloat16)
    vector = gather(handed, "panel", PANELS).transpose(1, 0, 2).reshape(16, U)
    (partial,) = over_columns(packs[2], 320, 0, 1, base=vector, dtype=jnp.float32)
    target = (solved_mine.astype(jnp.float32) - partial[0]).astype(jnp.bfloat16)
    smaller = [answer.reshape(2, SHARES, -1).transpose(1, 0, 2) for answer in answers]
    counts = [piece.shape[2] for piece in smaller]
    smaller = jnp.concatenate(smaller, 2)
    smaller = jnp.pad(smaller, ((0, 0), (0, 0), (0, ROWS - smaller.shape[2])))
    target = jnp.broadcast_to(target[None], (SHARES, 16, ROWS))
    got = exchange(jnp.concatenate([target, smaller], 1), SHARE)
    last = last_product(got, inverse_lower)
    lower_rows = share * ROWS + jnp.arange(ROWS, dtype=jnp.int32)
    lower_mask = (lower_rows // BLOCK < live_of(3)).astype(jnp.float32)[None, :]
    lower = scatter_sum(last.reshape(PANELS, 16, ROWS), "panel") * lower_mask

    got = got[:, 16:].transpose(1, 0, 2).astype(jnp.float32)
    outs = []
    start = 0
    for width in counts:
        outs.append(got[:, :, start : start + width])
        start += width
    return (outs[0], outs[1], outs[2], lower.reshape(2, SHARES, ROWS))


def solution(mesh):
    split = Mesh(mesh.devices.reshape(2, 2, 2, 4, 2, PANELS), LEAF + ("panel",))
    by_rows = P(None, "panel", LEAF)
    by_updates = P(None, LEAF, "panel")
    return jax.shard_map(
        shards,
        mesh=split,
        in_specs=(by_rows,) * 4 + (by_updates,) * 3 + (by_rows,) * 4 + (P(),) * 4,
        out_specs=(by_rows,) * 4,
        check_vma=False,
    )
```

```python
import functools

import jax
import jax.numpy as jnp
from jax import lax
from jax.experimental import pallas as pl
from jax.experimental.pallas import tpu as pltpu
from jax.sharding import Mesh
from jax.sharding import PartitionSpec as P

BLOCK = 128
P_SIZE = 5120
U = 2560
PANELS = 8
SHARES = 8
PIVOT_BLOCKS = P_SIZE // BLOCK
UPDATE_BLOCKS = U // BLOCK
ROWS = P_SIZE // PANELS
WIDE = 128

LEAF = ("z2", "z1", "z0", "x", "c")
SHARE = ("x", "c")
DEPTH = ("z2", "z1", "z0")


def exchange(value, axes):
    return lax.all_to_all(value, axes, 0, 0, tiled=True)


def scatter_sum(value, axes):
    return jnp.sum(exchange(value.astype(jnp.bfloat16), axes).astype(jnp.float32), 0)


def gather(value, axes, count):
    return exchange(jnp.broadcast_to(value[None], (count,) + value.shape), axes)


def partner(value):
    return lax.ppermute(value, "z0", [(0, 1), (1, 0)])


def halves(vector):
    half = vector.shape[0] // 2
    other = jnp.concatenate([vector[half:], -vector[:half]], 0)
    return vector.astype(jnp.bfloat16), other.astype(jnp.bfloat16)


def multiply(pieces, matrix_ref, start, span, contract):
    total = None
    for part, piece in enumerate(pieces):
        matrix = matrix_ref[start : start + span, part].reshape(ROWS, ROWS)
        if contract == 0:
            term = jnp.dot(piece, matrix, preferred_element_type=jnp.float32)
        else:
            dims = (((1,), (1,)), ((), ()))
            term = lax.dot_general(matrix, piece, dims, preferred_element_type=jnp.float32)
        total = term if total is None else total + term
    return total if contract == 0 else total.T


def bring(pack_ref, matrix_ref, sems, rows, offset):
    copies = []
    for share in range(SHARES):
        copies.append(
            pltpu.make_async_copy(
                pack_ref.at[share, :, pl.ds(offset * rows, rows)],
                matrix_ref.at[share],
                sems.at[share],
            )
        )
    for copy in copies:
        copy.start()
    return copies


def take_block(index_ref, held_ref, place):
    per = held_ref.shape[2] // BLOCK
    total = None
    for term in range(index_ref.shape[0]):
        spot = index_ref[term, place]
        safe = jnp.maximum(spot, 0)
        start = pl.multiple_of((safe % per) * BLOCK, BLOCK)
        block = held_ref[safe // per, :, pl.ds(start, BLOCK)].astype(jnp.float32)
        block = jnp.where(spot >= 0, block, 0.0)
        total = block if total is None else total + block
    return total


def params():
    return pltpu.CompilerParams(vmem_limit_bytes=24 * 2**20)


def smem():
    return pl.BlockSpec(memory_space=pltpu.SMEM)


def vmem():
    return pl.BlockSpec(memory_space=pltpu.VMEM)


def hbm():
    return pl.BlockSpec(memory_space=pltpu.HBM)


def in_hbm(value):
    return pltpu.with_memory_space_constraint(value, pltpu.HBM)


def matrix_scratch(rows):
    return [
        pltpu.VMEM((SHARES, 2, rows, ROWS), jnp.bfloat16),
        pltpu.SemaphoreType.DMA((SHARES,)),
    ]


def columns_kernel(rows, offset, updates, has_held, has_base, keep, *refs):
    refs = list(refs)
    index_ref = refs.pop(0) if has_held else None
    live_ref = refs.pop(0) if has_base and has_held else None
    held_ref = refs.pop(0) if has_held else None
    base_ref = refs.pop(0) if has_base else None
    pack_ref = refs.pop(0)
    out_ref = refs.pop(0)
    passed_ref = refs.pop(0) if updates else None
    keep_ref = refs.pop(0) if keep else None
    matrix_ref, sems = refs
    copies = bring(pack_ref, matrix_ref, sems, rows, offset)
    steps = SHARES * rows // ROWS
    span = ROWS // BLOCK
    group = ROWS // rows
    total = None
    for step in range(steps):
        if has_held:
            blocks = []
            for place in range(step * span, (step + 1) * span):
                block = take_block(index_ref, held_ref, place)
                if has_base:
                    base = base_ref[:, place * BLOCK : (place + 1) * BLOCK].astype(jnp.float32)
                    block = jnp.where(place < live_ref[0], base - block, 0.0)
                blocks.append(block)
            vector = jnp.concatenate(blocks, 1)
        else:
            vector = base_ref[:, step * ROWS : (step + 1) * ROWS].astype(jnp.float32)
        if keep:
            keep_ref[:, step * ROWS : (step + 1) * ROWS] = vector.astype(jnp.bfloat16)
        for share in range(step * group, (step + 1) * group):
            copies[share].wait()
        term = multiply(halves(vector), matrix_ref, step * group, group, 0)
        total = term if total is None else total + term
    for place in range(updates):
        passed_ref[:, place * BLOCK : (place + 1) * BLOCK] = take_block(
            index_ref, held_ref, steps * span + place
        )
    result = total.astype(out_ref.dtype)
    for copy in range(out_ref.shape[0]):
        out_ref[copy] = result


def over_columns(
    pack, rows, offset, copies, index=None, held=None, live=None, base=None,
    keep=False, dtype=jnp.bfloat16,
):
    steps = SHARES * rows // ROWS
    updates = index.shape[1] - steps * (ROWS // BLOCK) if index is not None else 0
    args, specs = [], []
    if held is not None:
        args.append(index)
        specs.append(smem())
        if base is not None:
            args.append(live)
            specs.append(smem())
        args.append(held)
        specs.append(vmem())
    if base is not None:
        args.append(base)
        specs.append(vmem())
    args.append(in_hbm(pack))
    specs.append(hbm())
    shapes = [jax.ShapeDtypeStruct((copies, 16, ROWS), dtype)]
    if updates:
        shapes.append(jax.ShapeDtypeStruct((16, updates * BLOCK), jnp.float32))
    if keep:
        shapes.append(jax.ShapeDtypeStruct((16, steps * ROWS), jnp.bfloat16))
    return pl.pallas_call(
        functools.partial(
            columns_kernel, rows, offset, updates, held is not None, base is not None, keep
        ),
        out_shape=shapes,
        in_specs=specs,
        out_specs=[vmem()] * len(shapes),
        scratch_shapes=matrix_scratch(rows),
        compiler_params=params(),
    )(*args)


def rows_kernel(rows, offset, parts, masked, *refs):
    refs = list(refs)
    live_ref = refs.pop(0) if masked else None
    part_refs = [refs.pop(0) for _ in range(parts)]
    held_ref = None if masked else refs.pop(0)
    pack_ref = refs.pop(0)
    out_ref = refs.pop(0)
    keep_ref = refs.pop(0) if masked else None
    matrix_ref, sems = refs
    copies = bring(pack_ref, matrix_ref, sems, rows, offset)
    total = None
    for part_ref in part_refs:
        for copy in range(part_ref.shape[0]):
            term = part_ref[copy].astype(jnp.float32)
            total = term if total is None else total + term
    if masked:
        place = lax.broadcasted_iota(jnp.int32, total.shape, 1) // BLOCK
        total = jnp.where(place < live_ref[0], total, 0.0)
        keep_ref[...] = total.astype(jnp.bfloat16)
    else:
        total = held_ref[...].astype(jnp.float32) - total
    pieces = halves(total)
    group = ROWS // rows
    for step in range(SHARES // group):
        for share in range(step * group, (step + 1) * group):
            copies[share].wait()
        result = multiply(pieces, matrix_ref, step * group, group, 1).astype(jnp.bfloat16)
        for copy in range(out_ref.shape[0]):
            out_ref[copy, :, step * ROWS : (step + 1) * ROWS] = result


def over_rows(pack, rows, offset, copies, parts, live=None, held=None):
    masked = live is not None
    args = ([live] if masked else []) + list(parts) + ([] if masked else [held]) + [in_hbm(pack)]
    specs = ([smem()] if masked else []) + [vmem()] * len(parts)
    specs += ([] if masked else [vmem()]) + [hbm()]
    shapes = [jax.ShapeDtypeStruct((copies, 16, SHARES * rows), jnp.bfloat16)]
    if masked:
        shapes.append(jax.ShapeDtypeStruct((16, ROWS), jnp.bfloat16))
    return pl.pallas_call(
        functools.partial(rows_kernel, rows, offset, len(parts), masked),
        out_shape=shapes,
        in_specs=specs,
        out_specs=[vmem()] * len(shapes),
        scratch_shapes=matrix_scratch(rows),
        compiler_params=params(),
    )(*args)


def crossed(vector):
    row = lax.broadcasted_iota(jnp.int32, (64, 64), 0)
    column = lax.broadcasted_iota(jnp.int32, (64, 64), 1)
    up = (column == row + 1) & (row % 2 == 0)
    down = (column == row - 1) & (row % 2 == 1)
    turn = jnp.where(up, 1.0, jnp.where(down, -1.0, 0.0)).astype(jnp.bfloat16)
    return jnp.dot(turn, vector, preferred_element_type=jnp.float32).astype(jnp.bfloat16)


def pair_dot(vector, other, matrix):
    dims = (((1,), (1,)), ((), ()))
    one = lax.dot_general(matrix[0], vector, dims, preferred_element_type=jnp.float32)
    two = lax.dot_general(matrix[1], other, dims, preferred_element_type=jnp.float32)
    return (one + two).T


def fetch(own_ref, matrix_ref, sem):
    copy = pltpu.make_async_copy(own_ref, matrix_ref, sem)
    copy.start()
    return copy


def lower_pivots_kernel(
    info_ref, every_ref, own_ref, other_ref, out_ref, matrix_ref, sems
):
    fetched = [
        fetch(own_ref, matrix_ref.at[0], sems.at[0]),
        fetch(other_ref, matrix_ref.at[1], sems.at[1]),
    ]
    place = lax.broadcasted_iota(jnp.int32, (64, ROWS), 1) // BLOCK
    sides = []
    for side in range(2):
        value = every_ref[side * 64 : (side + 1) * 64, :ROWS].astype(jnp.float32)
        sides.append(jnp.where(place + side * (ROWS // BLOCK) < info_ref[0], value, 0.0))
    even = info_ref[1] == 0
    vectors = (jnp.where(even, sides[0], sides[1]), jnp.where(even, sides[1], sides[0]))
    row = lax.broadcasted_iota(jnp.int32, (128, 128), 0)
    source = (row % 2) * 64 + (row // 2 % 8) * 8 + (row // 32) * 2 + row // 16 % 2
    order = (lax.broadcasted_iota(jnp.int32, (128, 128), 1) == source).astype(jnp.bfloat16)
    extra = jnp.dot(order, every_ref[:, ROWS:], preferred_element_type=jnp.float32)
    extra = extra.astype(jnp.bfloat16)
    total = None
    for side in range(2):
        vector = vectors[side].astype(jnp.bfloat16)
        turn = crossed(vector)
        fetched[side].wait()
        term = pair_dot(vector, turn, matrix_ref[side])
        total = term if total is None else total + term
    total = total.astype(jnp.bfloat16)
    for copy in range(4):
        out_ref[copy, :64] = total
        out_ref[copy, 64:] = extra[copy * 32 : (copy + 1) * 32]


def lower_pivots(info, every, own, other):
    return pl.pallas_call(
        lower_pivots_kernel,
        out_shape=jax.ShapeDtypeStruct((4, 96, ROWS), jnp.bfloat16),
        in_specs=[smem(), vmem(), hbm(), hbm()],
        out_specs=vmem(),
        scratch_shapes=[
            pltpu.VMEM((2,) + own.shape, jnp.bfloat16),
            pltpu.SemaphoreType.DMA((2,)),
        ],
        compiler_params=params(),
    )(info, every, in_hbm(own), in_hbm(other))


def lower_updates_kernel(
    info_ref, got_ref, own_ref, other_ref, out_ref, solved_ref, matrix_ref, sems
):
    fetched = [
        fetch(own_ref, matrix_ref.at[0], sems.at[0]),
        fetch(other_ref, matrix_ref.at[1], sems.at[1]),
    ]
    total = None
    for copy in range(4):
        term = got_ref[copy, :64].astype(jnp.float32)
        total = term if total is None else total + term
    place = lax.broadcasted_iota(jnp.int32, (64, ROWS), 1) // BLOCK
    vector = jnp.where(place < info_ref[0], total, 0.0).astype(jnp.bfloat16)
    solved_ref[...] = vector
    row = lax.broadcasted_iota(jnp.int32, (64, 64), 0)
    source = (row // 2 % 8) * 8 + (row // 16) * 2 + row % 2
    order = (lax.broadcasted_iota(jnp.int32, (64, 64), 1) == source).astype(jnp.bfloat16)
    vector = jnp.dot(order, vector, preferred_element_type=jnp.float32).astype(jnp.bfloat16)
    turn = crossed(vector)
    sides = []
    for side in range(2):
        fetched[side].wait()
        sides.append(pair_dot(vector, turn, matrix_ref[side]))
    even = info_ref[1] == 0
    own = sides[0].shape[1]
    first = jnp.where(even, sides[0], sides[1]).astype(jnp.bfloat16)
    second = jnp.where(even, sides[1], sides[0]).astype(jnp.bfloat16)
    for copy in range(2):
        out_ref[copy, :, :own] = first
        out_ref[copy, :, own:] = second


def lower_updates(info, got, own, other):
    return pl.pallas_call(
        lower_updates_kernel,
        out_shape=[
            jax.ShapeDtypeStruct((2, 64, ROWS), jnp.bfloat16),
            jax.ShapeDtypeStruct((64, ROWS), jnp.bfloat16),
        ],
        in_specs=[smem(), vmem(), hbm(), hbm()],
        out_specs=[vmem()] * 2,
        scratch_shapes=[
            pltpu.VMEM((2,) + own.shape, jnp.bfloat16),
            pltpu.SemaphoreType.DMA((2,)),
        ],
        compiler_params=params(),
    )(info, got, in_hbm(own), in_hbm(other))


def hand_kernel(masked, added, tailed, *refs):
    refs = list(refs)
    live_ref = refs.pop(0) if masked else None
    part_ref = refs.pop(0)
    more_ref = refs.pop(0) if added else None
    tail_ref = refs.pop(0) if tailed else None
    out_ref = refs.pop(0)
    total = part_ref[0].astype(jnp.float32)
    for copy in range(1, part_ref.shape[0]):
        total = total + part_ref[copy].astype(jnp.float32)
    if added:
        total = total + more_ref[...]
    if masked:
        place = lax.broadcasted_iota(jnp.int32, total.shape, 1) // BLOCK
        total = jnp.where(place < live_ref[0], total, 0.0)
    total = total.astype(jnp.bfloat16)
    for copy in range(out_ref.shape[0]):
        out_ref[copy, :, : total.shape[1]] = total
        if tailed:
            out_ref[copy, :, total.shape[1] :] = tail_ref[...]


def hand_on(part, copies, live=None, more=None, tail=None):
    width = part.shape[2] + (tail.shape[1] if tail is not None else 0)
    args = [item for item in (live, part, more, tail) if item is not None]
    specs = [smem()] * (live is not None) + [vmem()] * (len(args) - (live is not None))
    return pl.pallas_call(
        functools.partial(hand_kernel, live is not None, more is not None, tail is not None),
        out_shape=jax.ShapeDtypeStruct((copies, 16, width), jnp.bfloat16),
        in_specs=specs,
        out_specs=vmem(),
        compiler_params=params(),
    )(*args)


def pick_kernel(index_ref, held_ref, out_ref):
    for place in range(index_ref.shape[1]):
        out_ref[:, place * BLOCK : (place + 1) * BLOCK] = take_block(index_ref, held_ref, place)


def take_blocks(index, held):
    return pl.pallas_call(
        pick_kernel,
        out_shape=jax.ShapeDtypeStruct((held.shape[1], index.shape[1] * BLOCK), jnp.float32),
        in_specs=[smem(), pl.BlockSpec(memory_space=pltpu.VMEM)],
        out_specs=pl.BlockSpec(memory_space=pltpu.VMEM),
        compiler_params=params(),
    )(index, held)


def last_kernel(got_ref, own_ref, out_ref, matrix_ref, sem):
    fetched = fetch(own_ref, matrix_ref, sem)
    stacked = jnp.concatenate([got_ref[share, :16] for share in range(SHARES)], 0)
    row = lax.broadcasted_iota(jnp.int32, (WIDE, WIDE), 0)
    column = lax.broadcasted_iota(jnp.int32, (WIDE, WIDE), 1)
    total = None
    for part in range(2):
        imaginary = (row // 8 + part) % 2
        source = row % 8 * 16 + imaginary * 8 + row // 16
        sign = jnp.where((row // 8 % 2 == 1) & (part == 1), -1.0, 1.0)
        order = jnp.where(column == source, sign, 0.0).astype(jnp.bfloat16)
        vector = jnp.dot(order, stacked, preferred_element_type=jnp.float32)
        if part == 0:
            fetched.wait()
        term = jnp.dot(
            vector.astype(jnp.bfloat16), matrix_ref[part], preferred_element_type=jnp.float32
        )
        total = term if total is None else total + term
    out_ref[...] = total.astype(jnp.bfloat16)


def last_product(got, own):
    return pl.pallas_call(
        last_kernel,
        out_shape=jax.ShapeDtypeStruct((WIDE, ROWS), jnp.bfloat16),
        in_specs=[vmem(), hbm()],
        out_specs=vmem(),
        scratch_shapes=[pltpu.VMEM(own.shape, jnp.bfloat16), pltpu.SemaphoreType.DMA],
        compiler_params=params(),
    )(got, in_hbm(own))


def shards(
    inverse_root,
    inverse_upper,
    inverse_middle,
    inverse_lower,
    coupling_upper,
    coupling_middle,
    coupling_lower,
    source_root,
    source_upper,
    source_middle,
    source_lower,
    blocks_upper,
    blocks_middle,
    blocks_lower,
    live_blocks,
):
    tables = (None, blocks_upper, blocks_middle, blocks_lower)
    sources = (source_root, source_upper, source_middle, source_lower)
    depth = lax.axis_index(DEPTH)
    share = lax.axis_index(SHARE)
    column = lax.axis_index("panel")

    packs = [
        jnp.concatenate([inverse_middle.swapaxes(1, 2), coupling_middle], 1),
        jnp.concatenate([inverse_upper.swapaxes(1, 2), coupling_upper], 1),
        inverse_root.swapaxes(1, 2),
        coupling_lower,
    ]
    packs = [lax.all_gather(pack, SHARE, axis=0, tiled=False) for pack in packs]
    pivot_at = {2: (packs[0], 320, 0), 1: (packs[1], 160, 0), 0: (packs[2], 80, 0)}
    update_at = {2: (packs[0], 160, 2), 1: (packs[1], 80, 2)}

    def front_of(level):
        width = 8 >> level
        return depth // width, depth % width

    def live_of(level):
        front, _ = front_of(level)
        return lax.dynamic_slice_in_dim(live_blocks, (1 << level) - 1 + front, 1, 0)[0]

    def panel_live(level):
        return (live_of(level) - column * (ROWS // BLOCK))[None]

    def depth_live(level):
        return (live_of(level) - front_of(level)[1] * (PIVOT_BLOCKS // (8 >> level)))[None]

    def incoming(level):
        front, within = front_of(level)
        pair = lax.dynamic_slice_in_dim(tables[level + 1], 2 * front, 2, 0)
        pivots = PIVOT_BLOCKS // (8 >> level)
        goal = within * pivots + jnp.arange(pivots, dtype=jnp.int32)
        if level >= 1:
            updates = UPDATE_BLOCKS // (8 >> level)
            extra = PIVOT_BLOCKS + within * updates + jnp.arange(updates, dtype=jnp.int32)
            goal = jnp.concatenate([goal, extra])
        order = jnp.arange(2 * UPDATE_BLOCKS, dtype=jnp.int32).reshape(2, 1, UPDATE_BLOCKS)
        match = pair[:, None, :] == goal[None, :, None]
        return jnp.max(jnp.where(match, order, -1), 2)

    def picking(level, complete=False):
        front, within = front_of(level)
        parts = 16 >> level
        pivots = PIVOT_BLOCKS // parts
        updates = UPDATE_BLOCKS // parts if level >= 2 else 0
        own = UPDATE_BLOCKS // (8 >> level)
        row = lax.dynamic_slice_in_dim(tables[level], front, 1, 0)[0]
        if not complete:
            row = lax.dynamic_slice_in_dim(row, within * own, own, 0)
        whole = pivots + updates
        spot = row // pivots * whole + row % pivots
        if updates:
            rest = row - PIVOT_BLOCKS
            spot = jnp.where(rest >= 0, rest // updates * whole + pivots + rest % updates, spot)
        return spot[None]

    def handing():
        row = lax.dynamic_slice_in_dim(tables[3], depth, 1, 0)
        pivots = PIVOT_BLOCKS // 2
        updates = UPDATE_BLOCKS // 2
        rest = row - PIVOT_BLOCKS
        later = rest // updates * (pivots + updates) + pivots + rest % updates
        return jnp.where(rest >= 0, later, row // pivots * (pivots + updates) + row % pivots)

    core = lax.axis_index("c")
    other_inverse = lax.ppermute(inverse_lower, "c", [(0, 1), (1, 0)])
    other_coupling = lax.ppermute(coupling_lower, "c", [(0, 1), (1, 0)])
    packed = [source_lower] + [sources[level] for level in (2, 1, 0)]
    widths = [piece.shape[2] for piece in packed[1:]]
    packed = jnp.concatenate(packed, 2)
    packed = jnp.pad(packed, ((0, 0), (0, 0), (0, 2 * ROWS - packed.shape[2])))
    packed = packed.reshape(2, 4, 2, 2 * ROWS).transpose(2, 1, 0, 3).reshape(2, 1, 8, 2 * ROWS)
    packed = jnp.broadcast_to(packed, (2, PANELS, 8, 2 * ROWS)).reshape(16, 8, 2 * ROWS)
    every = exchange(packed, ("c", "panel")).reshape(WIDE, 2 * ROWS)
    place = lax.axis_index("x") * 2
    span = ROWS // BLOCK
    info = jnp.stack([live_of(3) - place * span, core])
    partial = lower_pivots(info, every, inverse_lower, other_inverse)
    got = exchange(partial, "x")
    info = jnp.stack([live_of(3) - column * span, core])
    update, solved = lower_updates(info, got, coupling_lower, other_coupling)
    solved_mine = lax.dynamic_slice_in_dim(
        solved.reshape(PANELS, 4, 2, ROWS), lax.axis_index("x"), 1, 1
    )
    solved_mine = solved_mine[:, 0].transpose(1, 0, 2).reshape(16, ROWS)

    children = exchange(update.reshape(64, 2, ROWS), ("z0", "x", "panel"))
    children = children.reshape(8, PANELS, 2, ROWS).astype(jnp.float32)
    children = jnp.sum(children, 1).astype(jnp.bfloat16)
    children = children.transpose(1, 0, 2).reshape(2, P_SIZE)
    spread = gather(children, "panel", PANELS).transpose(1, 0, 2).reshape(16, P_SIZE)
    gathered = spread[None]
    base = {}
    start = 0
    extra = got[:, 64:].reshape(4, 16, 2, ROWS).transpose(1, 0, 2, 3)
    for level, width in zip((2, 1, 0), widths):
        base[level] = extra[:, :, :, start : start + width].reshape(16, SHARES * width)
        start += width

    held = {}
    for level in (2, 1, 0):
        count = 8 >> level
        found = over_columns(
            *pivot_at[level],
            1 if level == 2 else count,
            index=incoming(level),
            held=gathered,
            live=depth_live(level),
            base=base[level],
        )
        if level == 2:
            parts = [found[0], partner(found[0])]
        else:
            parts = [exchange(found[0], DEPTH[level:])]
        if level >= 1:
            update, held[level] = over_rows(
                *update_at[level], PANELS, parts, live=panel_live(level)
            )
            update = hand_on(exchange(update, "panel"), 2 * count, more=found[1])
            gathered = exchange(update, DEPTH[level - 1 :])

    answers = []
    picked = None
    for level in (0, 1, 2):
        count = 8 >> level
        if level == 0:
            answer, _ = over_rows(*pivot_at[0], PANELS, parts, live=panel_live(0))
        else:
            partial, picked = over_columns(
                *update_at[level],
                1 if level == 2 else count,
                index=picking(level),
                held=gathered,
                keep=True,
            )
            if level == 2:
                parts = [partial, partner(partial)]
            else:
                parts = [exchange(partial, DEPTH[level:])]
            (answer,) = over_rows(
                *pivot_at[level], 1 if level == 2 else PANELS, parts, held=held[level]
            )
        if level < 2:
            outgoing = hand_on(
                exchange(answer, "panel"), count, live=depth_live(level), tail=picked
            )
            mine = outgoing[0, :, : P_SIZE // count].reshape(2, PANELS, -1)
            answers.append(lax.dynamic_slice_in_dim(mine, column, 1, 1)[:, 0])
            gathered = exchange(outgoing, DEPTH[level:])
        else:
            answer = answer.reshape(2, PANELS, -1).transpose(1, 0, 2)
            answer = exchange(jnp.concatenate([answer, answer], 0), ("z0", "panel"))
            answer = answer.reshape(2, PANELS, 2, -1).astype(jnp.float32)
            row_mask = (jnp.arange(P_SIZE, dtype=jnp.int32) // BLOCK < live_of(2)).reshape(2, 1, -1)
            both = (jnp.sum(answer, 1) * row_mask).astype(jnp.bfloat16)
            answers.append(lax.dynamic_slice_in_dim(both, front_of(2)[1], 1, 0)[0])

    passed = take_blocks(picking(2, True), gathered).reshape(2, PANELS, 2, -1)
    passed = lax.dynamic_slice_in_dim(passed, column, 1, 1)[:, 0].transpose(1, 0, 2)
    both = jnp.concatenate([both.astype(jnp.float32), passed], 2)
    handed = take_blocks(handing(), both).astype(jnp.bfloat16)
    vector = gather(handed, "panel", PANELS).transpose(1, 0, 2).reshape(16, U)
    (partial,) = over_columns(packs[3], 320, 0, 1, base=vector, dtype=jnp.float32)
    target = (solved_mine.astype(jnp.float32) - partial[0]).astype(jnp.bfloat16)
    smaller = [answer.reshape(2, SHARES, -1).transpose(1, 0, 2) for answer in answers]
    counts = [piece.shape[2] for piece in smaller]
    smaller = jnp.concatenate(smaller, 2)
    smaller = jnp.pad(smaller, ((0, 0), (0, 0), (0, ROWS - smaller.shape[2])))
    target = jnp.broadcast_to(target[None], (SHARES, 16, ROWS))
    got = exchange(jnp.concatenate([target, smaller], 1), SHARE)
    last = last_product(got, inverse_lower)
    lower_rows = share * ROWS + jnp.arange(ROWS, dtype=jnp.int32)
    lower_mask = (lower_rows // BLOCK < live_of(3)).astype(jnp.float32)[None, :]
    lower = scatter_sum(last.reshape(PANELS, 16, ROWS), "panel") * lower_mask

    got = got[:, 16:].transpose(1, 0, 2).astype(jnp.float32)
    outs = []
    start = 0
    for width in counts:
        outs.append(got[:, :, start : start + width])
        start += width
    return (outs[0], outs[1], outs[2], lower.reshape(2, SHARES, ROWS))


def solution(mesh):
    split = Mesh(mesh.devices.reshape(2, 2, 2, 4, 2, PANELS), LEAF + ("panel",))
    by_rows = P(None, "panel", LEAF)
    by_updates = P(None, LEAF, "panel")
    return jax.shard_map(
        shards,
        mesh=split,
        in_specs=(by_rows,) * 4 + (by_updates,) * 3 + (by_rows,) * 4 + (P(),) * 4,
        out_specs=(by_rows,) * 4,
        check_vma=False,
    )
```

```python
import functools

import jax
import jax.numpy as jnp
from jax import lax
from jax.experimental import pallas as pl
from jax.experimental.pallas import tpu as pltpu
from jax.sharding import Mesh
from jax.sharding import PartitionSpec as P

BLOCK = 128
P_SIZE = 5120
U = 2560
PANELS = 8
SHARES = 8
PIVOT_BLOCKS = P_SIZE // BLOCK
UPDATE_BLOCKS = U // BLOCK
ROWS = P_SIZE // PANELS
WIDE = 128

LEAF = ("z2", "z1", "z0", "x", "c")
SHARE = ("x", "c")
DEPTH = ("z2", "z1", "z0")


def exchange(value, axes):
    return lax.all_to_all(value, axes, 0, 0, tiled=True)


def scatter_sum(value, axes):
    return jnp.sum(exchange(value.astype(jnp.bfloat16), axes).astype(jnp.float32), 0)


def gather(value, axes, count):
    return exchange(jnp.broadcast_to(value[None], (count,) + value.shape), axes)


def partner(value):
    return lax.ppermute(value, "z0", [(0, 1), (1, 0)])


def halves(vector):
    half = vector.shape[0] // 2
    other = jnp.concatenate([vector[half:], -vector[:half]], 0)
    return vector.astype(jnp.bfloat16), other.astype(jnp.bfloat16)


def multiply(pieces, matrix_ref, start, span, contract, copies):
    total = None
    for part, piece in enumerate(pieces):
        for share in range(start, start + span):
            copies[share, part].wait()
        matrix = matrix_ref[start : start + span, part].reshape(ROWS, ROWS)
        if contract == 0:
            term = jnp.dot(piece, matrix, preferred_element_type=jnp.float32)
        else:
            dims = (((1,), (1,)), ((), ()))
            term = lax.dot_general(matrix, piece, dims, preferred_element_type=jnp.float32)
        total = term if total is None else total + term
    return total if contract == 0 else total.T


def bring(pack_ref, matrix_ref, sems, rows, offset):
    group = ROWS // rows
    copies = {}
    for first in range(0, SHARES, group):
        for part in range(2):
            for share in range(first, first + group):
                copy = pltpu.make_async_copy(
                    pack_ref.at[share, part, pl.ds(offset * rows, rows)],
                    matrix_ref.at[share, part],
                    sems.at[share, part],
                )
                copy.start()
                copies[share, part] = copy
    return copies


def take_block(index_ref, held_ref, place):
    per = held_ref.shape[2] // BLOCK
    total = None
    for term in range(index_ref.shape[0]):
        spot = index_ref[term, place]
        safe = jnp.maximum(spot, 0)
        start = pl.multiple_of((safe % per) * BLOCK, BLOCK)
        block = held_ref[safe // per, :, pl.ds(start, BLOCK)].astype(jnp.float32)
        block = jnp.where(spot >= 0, block, 0.0)
        total = block if total is None else total + block
    return total


def params():
    return pltpu.CompilerParams(vmem_limit_bytes=24 * 2**20)


def smem():
    return pl.BlockSpec(memory_space=pltpu.SMEM)


def vmem():
    return pl.BlockSpec(memory_space=pltpu.VMEM)


def hbm():
    return pl.BlockSpec(memory_space=pltpu.HBM)


def in_hbm(value):
    return pltpu.with_memory_space_constraint(value, pltpu.HBM)


def matrix_scratch(rows):
    return [
        pltpu.VMEM((SHARES, 2, rows, ROWS), jnp.bfloat16),
        pltpu.SemaphoreType.DMA((SHARES, 2)),
    ]


def columns_kernel(rows, offset, updates, has_held, has_base, keep, *refs):
    refs = list(refs)
    index_ref = refs.pop(0) if has_held else None
    live_ref = refs.pop(0) if has_base and has_held else None
    held_ref = refs.pop(0) if has_held else None
    base_ref = refs.pop(0) if has_base else None
    pack_ref = refs.pop(0)
    out_ref = refs.pop(0)
    passed_ref = refs.pop(0) if updates else None
    keep_ref = refs.pop(0) if keep else None
    matrix_ref, sems = refs
    copies = bring(pack_ref, matrix_ref, sems, rows, offset)
    steps = SHARES * rows // ROWS
    span = ROWS // BLOCK
    group = ROWS // rows
    total = None
    for step in range(steps):
        if has_held:
            blocks = []
            for place in range(step * span, (step + 1) * span):
                block = take_block(index_ref, held_ref, place)
                if has_base:
                    base = base_ref[:, place * BLOCK : (place + 1) * BLOCK].astype(jnp.float32)
                    block = jnp.where(place < live_ref[0], base - block, 0.0)
                blocks.append(block)
            vector = jnp.concatenate(blocks, 1)
        else:
            vector = base_ref[:, step * ROWS : (step + 1) * ROWS].astype(jnp.float32)
        if keep:
            keep_ref[:, step * ROWS : (step + 1) * ROWS] = vector.astype(jnp.bfloat16)
        term = multiply(halves(vector), matrix_ref, step * group, group, 0, copies)
        total = term if total is None else total + term
    for place in range(updates):
        passed_ref[:, place * BLOCK : (place + 1) * BLOCK] = take_block(
            index_ref, held_ref, steps * span + place
        )
    result = total.astype(out_ref.dtype)
    for copy in range(out_ref.shape[0]):
        out_ref[copy] = result


def over_columns(
    pack, rows, offset, copies, index=None, held=None, live=None, base=None,
    keep=False, dtype=jnp.bfloat16,
):
    steps = SHARES * rows // ROWS
    updates = index.shape[1] - steps * (ROWS // BLOCK) if index is not None else 0
    args, specs = [], []
    if held is not None:
        args.append(index)
        specs.append(smem())
        if base is not None:
            args.append(live)
            specs.append(smem())
        args.append(held)
        specs.append(vmem())
    if base is not None:
        args.append(base)
        specs.append(vmem())
    args.append(in_hbm(pack))
    specs.append(hbm())
    shapes = [jax.ShapeDtypeStruct((copies, 16, ROWS), dtype)]
    if updates:
        shapes.append(jax.ShapeDtypeStruct((16, updates * BLOCK), jnp.float32))
    if keep:
        shapes.append(jax.ShapeDtypeStruct((16, steps * ROWS), jnp.bfloat16))
    return pl.pallas_call(
        functools.partial(
            columns_kernel, rows, offset, updates, held is not None, base is not None, keep
        ),
        out_shape=shapes,
        in_specs=specs,
        out_specs=[vmem()] * len(shapes),
        scratch_shapes=matrix_scratch(rows),
        compiler_params=params(),
    )(*args)


def rows_kernel(rows, offset, parts, masked, *refs):
    refs = list(refs)
    live_ref = refs.pop(0) if masked else None
    part_refs = [refs.pop(0) for _ in range(parts)]
    held_ref = None if masked else refs.pop(0)
    pack_ref = refs.pop(0)
    out_ref = refs.pop(0)
    keep_ref = refs.pop(0) if masked else None
    matrix_ref, sems = refs
    copies = bring(pack_ref, matrix_ref, sems, rows, offset)
    total = None
    for part_ref in part_refs:
        for copy in range(part_ref.shape[0]):
            term = part_ref[copy].astype(jnp.float32)
            total = term if total is None else total + term
    if masked:
        place = lax.broadcasted_iota(jnp.int32, total.shape, 1) // BLOCK
        total = jnp.where(place < live_ref[0], total, 0.0)
        keep_ref[...] = total.astype(jnp.bfloat16)
    else:
        total = held_ref[...].astype(jnp.float32) - total
    pieces = halves(total)
    group = ROWS // rows
    for step in range(SHARES // group):
        result = multiply(pieces, matrix_ref, step * group, group, 1, copies)
        result = result.astype(jnp.bfloat16)
        for copy in range(out_ref.shape[0]):
            out_ref[copy, :, step * ROWS : (step + 1) * ROWS] = result


def over_rows(pack, rows, offset, copies, parts, live=None, held=None):
    masked = live is not None
    args = ([live] if masked else []) + list(parts) + ([] if masked else [held]) + [in_hbm(pack)]
    specs = ([smem()] if masked else []) + [vmem()] * len(parts)
    specs += ([] if masked else [vmem()]) + [hbm()]
    shapes = [jax.ShapeDtypeStruct((copies, 16, SHARES * rows), jnp.bfloat16)]
    if masked:
        shapes.append(jax.ShapeDtypeStruct((16, ROWS), jnp.bfloat16))
    return pl.pallas_call(
        functools.partial(rows_kernel, rows, offset, len(parts), masked),
        out_shape=shapes,
        in_specs=specs,
        out_specs=[vmem()] * len(shapes),
        scratch_shapes=matrix_scratch(rows),
        compiler_params=params(),
    )(*args)


def crossed(vector):
    row = lax.broadcasted_iota(jnp.int32, (64, 64), 0)
    column = lax.broadcasted_iota(jnp.int32, (64, 64), 1)
    up = (column == row + 1) & (row % 2 == 0)
    down = (column == row - 1) & (row % 2 == 1)
    turn = jnp.where(up, 1.0, jnp.where(down, -1.0, 0.0)).astype(jnp.bfloat16)
    return jnp.dot(turn, vector, preferred_element_type=jnp.float32).astype(jnp.bfloat16)


def pair_dot(vector, other, matrix):
    dims = (((1,), (1,)), ((), ()))
    one = lax.dot_general(matrix[0], vector, dims, preferred_element_type=jnp.float32)
    two = lax.dot_general(matrix[1], other, dims, preferred_element_type=jnp.float32)
    return (one + two).T


def fetch(own_ref, matrix_ref, sem):
    copy = pltpu.make_async_copy(own_ref, matrix_ref, sem)
    copy.start()
    return copy


def lower_pivots_kernel(
    info_ref, every_ref, own_ref, other_ref, out_ref, matrix_ref, sems
):
    fetched = [
        fetch(own_ref, matrix_ref.at[0], sems.at[0]),
        fetch(other_ref, matrix_ref.at[1], sems.at[1]),
    ]
    place = lax.broadcasted_iota(jnp.int32, (64, ROWS), 1) // BLOCK
    sides = []
    for side in range(2):
        value = every_ref[side * 64 : (side + 1) * 64, :ROWS].astype(jnp.float32)
        sides.append(jnp.where(place + side * (ROWS // BLOCK) < info_ref[0], value, 0.0))
    even = info_ref[1] == 0
    vectors = (jnp.where(even, sides[0], sides[1]), jnp.where(even, sides[1], sides[0]))
    row = lax.broadcasted_iota(jnp.int32, (128, 128), 0)
    source = (row % 2) * 64 + (row // 2 % 8) * 8 + (row // 32) * 2 + row // 16 % 2
    order = (lax.broadcasted_iota(jnp.int32, (128, 128), 1) == source).astype(jnp.bfloat16)
    extra = jnp.dot(order, every_ref[:, ROWS:], preferred_element_type=jnp.float32)
    extra = extra.astype(jnp.bfloat16)
    total = None
    for side in range(2):
        vector = vectors[side].astype(jnp.bfloat16)
        turn = crossed(vector)
        fetched[side].wait()
        term = pair_dot(vector, turn, matrix_ref[side])
        total = term if total is None else total + term
    total = total.astype(jnp.bfloat16)
    for copy in range(4):
        out_ref[copy, :64] = total
        out_ref[copy, 64:] = extra[copy * 32 : (copy + 1) * 32]


def lower_pivots(info, every, own, other):
    return pl.pallas_call(
        lower_pivots_kernel,
        out_shape=jax.ShapeDtypeStruct((4, 96, ROWS), jnp.bfloat16),
        in_specs=[smem(), vmem(), hbm(), hbm()],
        out_specs=vmem(),
        scratch_shapes=[
            pltpu.VMEM((2,) + own.shape, jnp.bfloat16),
            pltpu.SemaphoreType.DMA((2,)),
        ],
        compiler_params=params(),
    )(info, every, in_hbm(own), in_hbm(other))


def lower_updates_kernel(
    info_ref, got_ref, own_ref, other_ref, out_ref, solved_ref, matrix_ref, sems
):
    fetched = [
        fetch(own_ref, matrix_ref.at[0], sems.at[0]),
        fetch(other_ref, matrix_ref.at[1], sems.at[1]),
    ]
    total = None
    for copy in range(4):
        term = got_ref[copy, :64].astype(jnp.float32)
        total = term if total is None else total + term
    place = lax.broadcasted_iota(jnp.int32, (64, ROWS), 1) // BLOCK
    vector = jnp.where(place < info_ref[0], total, 0.0).astype(jnp.bfloat16)
    solved_ref[...] = vector
    row = lax.broadcasted_iota(jnp.int32, (64, 64), 0)
    source = (row // 2 % 8) * 8 + (row // 16) * 2 + row % 2
    order = (lax.broadcasted_iota(jnp.int32, (64, 64), 1) == source).astype(jnp.bfloat16)
    vector = jnp.dot(order, vector, preferred_element_type=jnp.float32).astype(jnp.bfloat16)
    turn = crossed(vector)
    sides = []
    for side in range(2):
        fetched[side].wait()
        sides.append(pair_dot(vector, turn, matrix_ref[side]))
    even = info_ref[1] == 0
    own = sides[0].shape[1]
    first = jnp.where(even, sides[0], sides[1]).astype(jnp.bfloat16)
    second = jnp.where(even, sides[1], sides[0]).astype(jnp.bfloat16)
    for copy in range(2):
        out_ref[copy, :, :own] = first
        out_ref[copy, :, own:] = second


def lower_updates(info, got, own, other):
    return pl.pallas_call(
        lower_updates_kernel,
        out_shape=[
            jax.ShapeDtypeStruct((2, 64, ROWS), jnp.bfloat16),
            jax.ShapeDtypeStruct((64, ROWS), jnp.bfloat16),
        ],
        in_specs=[smem(), vmem(), hbm(), hbm()],
        out_specs=[vmem()] * 2,
        scratch_shapes=[
            pltpu.VMEM((2,) + own.shape, jnp.bfloat16),
            pltpu.SemaphoreType.DMA((2,)),
        ],
        compiler_params=params(),
    )(info, got, in_hbm(own), in_hbm(other))


def hand_kernel(masked, added, tailed, *refs):
    refs = list(refs)
    live_ref = refs.pop(0) if masked else None
    part_ref = refs.pop(0)
    more_ref = refs.pop(0) if added else None
    tail_ref = refs.pop(0) if tailed else None
    out_ref = refs.pop(0)
    total = part_ref[0].astype(jnp.float32)
    for copy in range(1, part_ref.shape[0]):
        total = total + part_ref[copy].astype(jnp.float32)
    if added:
        total = total + more_ref[...]
    if masked:
        place = lax.broadcasted_iota(jnp.int32, total.shape, 1) // BLOCK
        total = jnp.where(place < live_ref[0], total, 0.0)
    total = total.astype(jnp.bfloat16)
    for copy in range(out_ref.shape[0]):
        out_ref[copy, :, : total.shape[1]] = total
        if tailed:
            out_ref[copy, :, total.shape[1] :] = tail_ref[...]


def hand_on(part, copies, live=None, more=None, tail=None):
    width = part.shape[2] + (tail.shape[1] if tail is not None else 0)
    args = [item for item in (live, part, more, tail) if item is not None]
    specs = [smem()] * (live is not None) + [vmem()] * (len(args) - (live is not None))
    return pl.pallas_call(
        functools.partial(hand_kernel, live is not None, more is not None, tail is not None),
        out_shape=jax.ShapeDtypeStruct((copies, 16, width), jnp.bfloat16),
        in_specs=specs,
        out_specs=vmem(),
        compiler_params=params(),
    )(*args)


def pick_kernel(index_ref, held_ref, out_ref):
    for place in range(index_ref.shape[1]):
        out_ref[:, place * BLOCK : (place + 1) * BLOCK] = take_block(index_ref, held_ref, place)


def take_blocks(index, held):
    return pl.pallas_call(
        pick_kernel,
        out_shape=jax.ShapeDtypeStruct((held.shape[1], index.shape[1] * BLOCK), jnp.float32),
        in_specs=[smem(), pl.BlockSpec(memory_space=pltpu.VMEM)],
        out_specs=pl.BlockSpec(memory_space=pltpu.VMEM),
        compiler_params=params(),
    )(index, held)


def last_kernel(got_ref, own_ref, out_ref, matrix_ref, sem):
    fetched = fetch(own_ref, matrix_ref, sem)
    stacked = jnp.concatenate([got_ref[share, :16] for share in range(SHARES)], 0)
    row = lax.broadcasted_iota(jnp.int32, (WIDE, WIDE), 0)
    column = lax.broadcasted_iota(jnp.int32, (WIDE, WIDE), 1)
    total = None
    for part in range(2):
        imaginary = (row // 8 + part) % 2
        source = row % 8 * 16 + imaginary * 8 + row // 16
        sign = jnp.where((row // 8 % 2 == 1) & (part == 1), -1.0, 1.0)
        order = jnp.where(column == source, sign, 0.0).astype(jnp.bfloat16)
        vector = jnp.dot(order, stacked, preferred_element_type=jnp.float32)
        if part == 0:
            fetched.wait()
        term = jnp.dot(
            vector.astype(jnp.bfloat16), matrix_ref[part], preferred_element_type=jnp.float32
        )
        total = term if total is None else total + term
    out_ref[...] = total.astype(jnp.bfloat16)


def last_product(got, own):
    return pl.pallas_call(
        last_kernel,
        out_shape=jax.ShapeDtypeStruct((WIDE, ROWS), jnp.bfloat16),
        in_specs=[vmem(), hbm()],
        out_specs=vmem(),
        scratch_shapes=[pltpu.VMEM(own.shape, jnp.bfloat16), pltpu.SemaphoreType.DMA],
        compiler_params=params(),
    )(got, in_hbm(own))


def shards(
    inverse_root,
    inverse_upper,
    inverse_middle,
    inverse_lower,
    coupling_upper,
    coupling_middle,
    coupling_lower,
    source_root,
    source_upper,
    source_middle,
    source_lower,
    blocks_upper,
    blocks_middle,
    blocks_lower,
    live_blocks,
):
    tables = (None, blocks_upper, blocks_middle, blocks_lower)
    sources = (source_root, source_upper, source_middle, source_lower)
    depth = lax.axis_index(DEPTH)
    share = lax.axis_index(SHARE)
    column = lax.axis_index("panel")

    packs = [
        jnp.concatenate([inverse_middle.swapaxes(1, 2), coupling_middle], 1),
        jnp.concatenate([inverse_upper.swapaxes(1, 2), coupling_upper], 1),
        inverse_root.swapaxes(1, 2),
        coupling_lower,
    ]
    packs = [lax.all_gather(pack, SHARE, axis=0, tiled=False) for pack in packs]
    pivot_at = {2: (packs[0], 320, 0), 1: (packs[1], 160, 0), 0: (packs[2], 80, 0)}
    update_at = {2: (packs[0], 160, 2), 1: (packs[1], 80, 2)}

    def front_of(level):
        width = 8 >> level
        return depth // width, depth % width

    def live_of(level):
        front, _ = front_of(level)
        return lax.dynamic_slice_in_dim(live_blocks, (1 << level) - 1 + front, 1, 0)[0]

    def panel_live(level):
        return (live_of(level) - column * (ROWS // BLOCK))[None]

    def depth_live(level):
        return (live_of(level) - front_of(level)[1] * (PIVOT_BLOCKS // (8 >> level)))[None]

    def incoming(level):
        front, within = front_of(level)
        pair = lax.dynamic_slice_in_dim(tables[level + 1], 2 * front, 2, 0)
        pivots = PIVOT_BLOCKS // (8 >> level)
        goal = within * pivots + jnp.arange(pivots, dtype=jnp.int32)
        if level >= 1:
            updates = UPDATE_BLOCKS // (8 >> level)
            extra = PIVOT_BLOCKS + within * updates + jnp.arange(updates, dtype=jnp.int32)
            goal = jnp.concatenate([goal, extra])
        order = jnp.arange(2 * UPDATE_BLOCKS, dtype=jnp.int32).reshape(2, 1, UPDATE_BLOCKS)
        match = pair[:, None, :] == goal[None, :, None]
        return jnp.max(jnp.where(match, order, -1), 2)

    def picking(level, complete=False):
        front, within = front_of(level)
        parts = 16 >> level
        pivots = PIVOT_BLOCKS // parts
        updates = UPDATE_BLOCKS // parts if level >= 2 else 0
        own = UPDATE_BLOCKS // (8 >> level)
        row = lax.dynamic_slice_in_dim(tables[level], front, 1, 0)[0]
        if not complete:
            row = lax.dynamic_slice_in_dim(row, within * own, own, 0)
        whole = pivots + updates
        spot = row // pivots * whole + row % pivots
        if updates:
            rest = row - PIVOT_BLOCKS
            spot = jnp.where(rest >= 0, rest // updates * whole + pivots + rest % updates, spot)
        return spot[None]

    def handing():
        row = lax.dynamic_slice_in_dim(tables[3], depth, 1, 0)
        pivots = PIVOT_BLOCKS // 2
        updates = UPDATE_BLOCKS // 2
        rest = row - PIVOT_BLOCKS
        later = rest // updates * (pivots + updates) + pivots + rest % updates
        return jnp.where(rest >= 0, later, row // pivots * (pivots + updates) + row % pivots)

    core = lax.axis_index("c")
    other_inverse = lax.ppermute(inverse_lower, "c", [(0, 1), (1, 0)])
    other_coupling = lax.ppermute(coupling_lower, "c", [(0, 1), (1, 0)])
    packed = [source_lower] + [sources[level] for level in (2, 1, 0)]
    widths = [piece.shape[2] for piece in packed[1:]]
    packed = jnp.concatenate(packed, 2)
    packed = jnp.pad(packed, ((0, 0), (0, 0), (0, 2 * ROWS - packed.shape[2])))
    packed = packed.reshape(2, 4, 2, 2 * ROWS).transpose(2, 1, 0, 3).reshape(2, 1, 8, 2 * ROWS)
    packed = jnp.broadcast_to(packed, (2, PANELS, 8, 2 * ROWS)).reshape(16, 8, 2 * ROWS)
    every = exchange(packed, ("c", "panel")).reshape(WIDE, 2 * ROWS)
    place = lax.axis_index("x") * 2
    span = ROWS // BLOCK
    info = jnp.stack([live_of(3) - place * span, core])
    partial = lower_pivots(info, every, inverse_lower, other_inverse)
    got = exchange(partial, "x")
    info = jnp.stack([live_of(3) - column * span, core])
    update, solved = lower_updates(info, got, coupling_lower, other_coupling)
    solved_mine = lax.dynamic_slice_in_dim(
        solved.reshape(PANELS, 4, 2, ROWS), lax.axis_index("x"), 1, 1
    )
    solved_mine = solved_mine[:, 0].transpose(1, 0, 2).reshape(16, ROWS)

    children = exchange(update.reshape(64, 2, ROWS), ("z0", "x", "panel"))
    children = children.reshape(8, PANELS, 2, ROWS).astype(jnp.float32)
    children = jnp.sum(children, 1).astype(jnp.bfloat16)
    children = children.transpose(1, 0, 2).reshape(2, P_SIZE)
    spread = gather(children, "panel", PANELS).transpose(1, 0, 2).reshape(16, P_SIZE)
    gathered = spread[None]
    base = {}
    start = 0
    extra = got[:, 64:].reshape(4, 16, 2, ROWS).transpose(1, 0, 2, 3)
    for level, width in zip((2, 1, 0), widths):
        base[level] = extra[:, :, :, start : start + width].reshape(16, SHARES * width)
        start += width

    held = {}
    for level in (2, 1, 0):
        count = 8 >> level
        found = over_columns(
            *pivot_at[level],
            1 if level == 2 else count,
            index=incoming(level),
            held=gathered,
            live=depth_live(level),
            base=base[level],
        )
        if level == 2:
            parts = [found[0], partner(found[0])]
        else:
            parts = [exchange(found[0], DEPTH[level:])]
        if level >= 1:
            update, held[level] = over_rows(
                *update_at[level], PANELS, parts, live=panel_live(level)
            )
            update = hand_on(exchange(update, "panel"), 2 * count, more=found[1])
            gathered = exchange(update, DEPTH[level - 1 :])

    answers = []
    picked = None
    for level in (0, 1, 2):
        count = 8 >> level
        if level == 0:
            answer, _ = over_rows(*pivot_at[0], PANELS, parts, live=panel_live(0))
        else:
            partial, picked = over_columns(
                *update_at[level],
                1 if level == 2 else count,
                index=picking(level),
                held=gathered,
                keep=True,
            )
            if level == 2:
                parts = [partial, partner(partial)]
            else:
                parts = [exchange(partial, DEPTH[level:])]
            (answer,) = over_rows(
                *pivot_at[level], 1 if level == 2 else PANELS, parts, held=held[level]
            )
        if level < 2:
            outgoing = hand_on(
                exchange(answer, "panel"), count, live=depth_live(level), tail=picked
            )
            mine = outgoing[0, :, : P_SIZE // count].reshape(2, PANELS, -1)
            answers.append(lax.dynamic_slice_in_dim(mine, column, 1, 1)[:, 0])
            gathered = exchange(outgoing, DEPTH[level:])
        else:
            answer = answer.reshape(2, PANELS, -1).transpose(1, 0, 2)
            answer = exchange(jnp.concatenate([answer, answer], 0), ("z0", "panel"))
            answer = answer.reshape(2, PANELS, 2, -1).astype(jnp.float32)
            row_mask = (jnp.arange(P_SIZE, dtype=jnp.int32) // BLOCK < live_of(2)).reshape(2, 1, -1)
            both = (jnp.sum(answer, 1) * row_mask).astype(jnp.bfloat16)
            answers.append(lax.dynamic_slice_in_dim(both, front_of(2)[1], 1, 0)[0])

    passed = take_blocks(picking(2, True), gathered).reshape(2, PANELS, 2, -1)
    passed = lax.dynamic_slice_in_dim(passed, column, 1, 1)[:, 0].transpose(1, 0, 2)
    both = jnp.concatenate([both.astype(jnp.float32), passed], 2)
    handed = take_blocks(handing(), both).astype(jnp.bfloat16)
    vector = gather(handed, "panel", PANELS).transpose(1, 0, 2).reshape(16, U)
    (partial,) = over_columns(packs[3], 320, 0, 1, base=vector, dtype=jnp.float32)
    target = (solved_mine.astype(jnp.float32) - partial[0]).astype(jnp.bfloat16)
    smaller = [answer.reshape(2, SHARES, -1).transpose(1, 0, 2) for answer in answers]
    counts = [piece.shape[2] for piece in smaller]
    smaller = jnp.concatenate(smaller, 2)
    smaller = jnp.pad(smaller, ((0, 0), (0, 0), (0, ROWS - smaller.shape[2])))
    target = jnp.broadcast_to(target[None], (SHARES, 16, ROWS))
    got = exchange(jnp.concatenate([target, smaller], 1), SHARE)
    last = last_product(got, inverse_lower)
    lower_rows = share * ROWS + jnp.arange(ROWS, dtype=jnp.int32)
    lower_mask = (lower_rows // BLOCK < live_of(3)).astype(jnp.float32)[None, :]
    lower = scatter_sum(last.reshape(PANELS, 16, ROWS), "panel") * lower_mask

    got = got[:, 16:].transpose(1, 0, 2).astype(jnp.float32)
    outs = []
    start = 0
    for width in counts:
        outs.append(got[:, :, start : start + width])
        start += width
    return (outs[0], outs[1], outs[2], lower.reshape(2, SHARES, ROWS))


def solution(mesh):
    split = Mesh(mesh.devices.reshape(2, 2, 2, 4, 2, PANELS), LEAF + ("panel",))
    by_rows = P(None, "panel", LEAF)
    by_updates = P(None, LEAF, "panel")
    return jax.shard_map(
        shards,
        mesh=split,
        in_specs=(by_rows,) * 4 + (by_updates,) * 3 + (by_rows,) * 4 + (P(),) * 4,
        out_specs=(by_rows,) * 4,
        check_vma=False,
    )
```
